32 devices in a mesh: pitch: 8 (over z, x), span: 4 (over y, core).
Axes of the slice: x: 2, y: 2, z: 4, core: 2. Of those that a mesh axis runs over, the one named last changes fastest.
Arguments:
- adjoint: float32 [5, 32, 64, 256], P(None, 'pitch', 'span'), may hold values from -6 to 6
- gradient: float32 [5, 32, 64, 256], P(None, 'pitch', 'span'), may hold values from -6 to 6
- diag_blocks: bfloat16 [5, 5, 32, 64, 256], P(None, None, 'pitch', 'span')
- off_blocks: bfloat16 [6, 5, 5, 32, 64, 256], P(None, None, None, 'pitch', 'span'), may hold values from -2.5 to 2.5
- precond: bfloat16 [5, 5, 32, 64, 256], P(None, None, 'pitch', 'span')
- low_donor: int32 [64, 256, 2], P('span'), may hold values from 0 to 4095
- low_weight: float32 [64, 256, 2], P('span'), may hold values from 0.2 to 1
- high_donor: int32 [64, 256, 2], P('span'), may hold values from 0 to 4095
- high_weight: float32 [64, 256, 2], P('span'), may hold values from 0.2 to 1
- tip_mask: int32 [32, 64, 256], P('pitch', 'span'), may hold values 0 or 1
Outputs:
- adjoint_out: float32 [5, 32, 64, 256], P(None, 'pitch', 'span')
The draws below stay inside these ranges and needn't reach their ends.
Inputs may be any that keep to these rules, and one draw needn't show every extreme that they name: `low_donor`: each id names a cell of the opposite pitch end within the span rows of the receiving cell's span block of 16 rows. `high_donor`: each id names a cell of the opposite pitch end within the span rows of the receiving cell's span block of 16 rows.
All inputs are finite; a program needn't handle non-finite values. No bound on the sum of `tip_mask` on one device may be relied on, other than what follows from the above.
Results may differ from the reference program's by a relative error of at most 0.0003.
Values sent between devices are 32-bit elements; how exact they have to be, the bound alone decides.
A program may use at most 64 MiB of HBM per device.

```python
import jax
import jax.numpy as jnp
from jax import lax

NV = 5
INTERSECTIONS = 2
ITERS = 2
CS = 16
NX = 256
NP = 32
NS = 64


def draw_diag_blocks(key, part):
    key = jax.random.fold_in(key, 11)
    noise = 0.3 * jax.random.normal(key, (NV, NV, NP, NS, NX), jnp.float32)
    identity = jnp.eye(NV, dtype=jnp.float32)[:, :, None, None, None]
    return (4.0 * identity + noise).astype(jnp.bfloat16)


def draw_precond(key, part):
    key = jax.random.fold_in(key, 23)
    noise = 0.03 * jax.random.normal(key, (NV, NV, NP, NS, NX), jnp.float32)
    identity = jnp.eye(NV, dtype=jnp.float32)[:, :, None, None, None]
    return (0.25 * identity + noise).astype(jnp.bfloat16)


def touch_ends(result, stream_key, low, top_value):
    extent = result.shape
    place = [jax.random.randint(jax.random.fold_in(stream_key, axis), (), 0, extent[axis]) for axis in range(len(extent))]
    result = result.at[tuple(place)].set(low)
    longest = extent.index(max(extent))
    place[longest] = (place[longest] + 1) % extent[longest]
    return result.at[tuple(place)].set(top_value)


def shard_levels(stream_key, shape, split, low, largest):
    factor_of, own = 1.0, jax.random.fold_in(stream_key, 6)
    for axis_at, blocks in split:
        draws = jnp.exp(jax.random.uniform(jax.random.fold_in(own, axis_at), (blocks,), jnp.float32, low / len(split), largest / len(split)))
        factor_of = factor_of * jnp.repeat(draws, shape[axis_at] // blocks).reshape([-1 if axis == axis_at else 1 for axis in range(len(shape))])
    return factor_of


def gaussian(own_key, extent, scale, reach, shards=(), held_as=jnp.bfloat16):
    values = jax.random.normal(own_key, extent, jnp.float32) * scale
    if len(shards) > 0:
        values = shard_levels(own_key, extent, shards, -0.22, 0.18) * values
    return jnp.clip(values, min=-reach, max=reach).astype(held_as)


def setup_inputs(seed: int = 0) -> dict:
    splits = jax.random.split(jax.random.key(seed), 11)
    return {
        "adjoint": gaussian(splits[0], (NV, NP, NS, NX), 1.0, 6.0, ((1, 8), (2, 4)), jnp.float32),
        "gradient": gaussian(splits[1], (NV, NP, NS, NX), 1.0, 6.0, ((1, 8), (2, 4)), jnp.float32),
        "diag_blocks": draw_diag_blocks(jax.random.fold_in(splits[10], 71), 0),
        "off_blocks": gaussian(splits[3], (6, NV, NV, NP, NS, NX), 0.3, 2.5, ((3, 8), (4, 4))),
        "precond": draw_precond(jax.random.fold_in(splits[10], 71), 0),
        "low_donor": touch_ends(jax.random.randint(splits[5], (NS, NX, INTERSECTIONS), 0, CS * NX), jax.random.fold_in(splits[5], 1), 0, (CS * NX) - 1).astype(jnp.int32),
        "low_weight": jnp.clip(0.2 + 0.8 * jax.random.uniform(splits[6], (NS, NX, INTERSECTIONS), jnp.float32) ** shard_levels(splits[6], (NS, NX, INTERSECTIONS), ((0, 4),), -0.2, 0.2), 0.2, 1.0),
        "high_donor": touch_ends(jax.random.randint(splits[7], (NS, NX, INTERSECTIONS), 0, CS * NX), jax.random.fold_in(splits[7], 1), 0, (CS * NX) - 1).astype(jnp.int32),
        "high_weight": jnp.clip(0.2 + 0.8 * jax.random.uniform(splits[8], (NS, NX, INTERSECTIONS), jnp.float32) ** shard_levels(splits[8], (NS, NX, INTERSECTIONS), ((0, 4),), -0.2, 0.2), 0.2, 1.0),
        "tip_mask": touch_ends((jax.random.randint(splits[9], (NP, NS, NX), 0, 8) < 1).astype(jnp.int32), jax.random.fold_in(splits[9], 1), 0, 1),
    }


def shift_forward(field, axis):
    widths = [(0, 0)] * field.ndim
    widths[axis] = (1, 0)
    return lax.slice_in_dim(jnp.pad(field, widths), 0, field.shape[axis], axis=axis)


def shift_backward(field, axis):
    widths = [(0, 0)] * field.ndim
    widths[axis] = (0, 1)
    return lax.slice_in_dim(jnp.pad(field, widths), 1, field.shape[axis] + 1, axis=axis)


def scatter_face(values, donors, weights):
    span_rows = jnp.arange(NS, dtype=jnp.int32)[:, None, None]
    global_ids = (span_rows // CS) * (CS * NX) + donors
    spread = values[:, :, :, None] * weights[None]
    summed = jax.ops.segment_sum(spread.reshape(NV, -1).T, global_ids.reshape(-1), num_segments=NS * NX)
    return summed.T.reshape(NV, NS, NX)


def reference(adjoint, gradient, diag_blocks, off_blocks, precond, low_donor, low_weight, high_donor, high_weight, tip_mask):
    highest = lax.Precision.HIGHEST
    step_size = jnp.where(tip_mask == 1, 0.3, 0.6).astype(jnp.float32)
    for sweep in range(ITERS):
        outgoing = jnp.einsum('dabpsx,apsx->dbpsx', off_blocks.astype(jnp.float32), adjoint, precision=highest)
        applied = jnp.einsum('abpsx,apsx->bpsx', diag_blocks.astype(jnp.float32), adjoint, precision=highest)
        applied = applied + shift_backward(outgoing[0], 1) + shift_forward(outgoing[1], 1)
        applied = applied + shift_backward(outgoing[2], 2) + shift_forward(outgoing[3], 2)
        applied = applied + shift_backward(outgoing[4], 3) + shift_forward(outgoing[5], 3)
        to_high = scatter_face(outgoing[0][:, 0], low_donor, low_weight)
        to_low = scatter_face(outgoing[1][:, NP - 1], high_donor, high_weight)
        applied = applied.at[:, NP - 1].add(to_high)
        applied = applied.at[:, 0].add(to_low)
        update = jnp.einsum('abpsx,bpsx->apsx', precond.astype(jnp.float32), applied + gradient, precision=highest)
        adjoint = adjoint - step_size[None] * update
    return adjoint
```

```python
import functools

import jax
import jax.numpy as jnp
from jax import lax
from jax.experimental import pallas as pl
from jax.experimental.pallas import tpu as pltpu
from jax.sharding import PartitionSpec as P

ITERS = 2
MESH = pl.DeviceIdType.MESH
UNROLL = 4


def kernel(
    dims,
    adj_h, grad_h, diag_h, off_h, pre_h, ld_h, lw_h, hd_h, hw_h, tip_h,
    out,
    adj, grad, diag, off, pre, tabd, tabw, tip,
    onehot, face, scat, acc,
    s_up, s_dn, r_up, r_dn, s_left, s_right, r_left, r_right,
    load_sem, send_sem, recv_sem,
):
    pitches, spans, nv, lp, rows, nx, entries = dims
    top = lp - 1
    bits = nx.bit_length() - 1
    pi = lax.axis_index("pitch")
    si = lax.axis_index("span")
    above = lax.rem(pi + 1, pitches)
    below = lax.rem(pi + pitches - 1, pitches)
    is_first = pi == 0
    is_last = pi == pitches - 1
    is_end = jnp.logical_or(is_first, is_last)
    has_left = si > 0
    has_right = si < spans - 1

    barrier = pltpu.get_barrier_semaphore()
    pl.semaphore_signal(barrier, inc=1, device_id={"pitch": above}, device_id_type=MESH)
    pl.semaphore_signal(barrier, inc=1, device_id={"pitch": below}, device_id_type=MESH)

    @pl.when(has_left)
    def _():
        pl.semaphore_signal(barrier, inc=1, device_id={"span": si - 1}, device_id_type=MESH)

    @pl.when(has_right)
    def _():
        pl.semaphore_signal(barrier, inc=1, device_id={"span": si + 1}, device_id_type=MESH)

    def load(src, dst, n):
        return pltpu.make_async_copy(src, dst, load_sem.at[n])

    low_d, low_w = load(ld_h, tabd, 0), load(lw_h, tabw, 1)
    high_d, high_w = load(hd_h, tabd, 0), load(hw_h, tabw, 1)
    faces = [
        load(adj_h, adj, 2),
        load(off_h.at[0, :, :, 0], off.at[0, :, :, 0], 3),
        load(off_h.at[1, :, :, top], off.at[1, :, :, top], 4),
    ]
    span_part = [load(off_h.at[2], off.at[2], 5), load(off_h.at[3], off.at[3], 6)]
    rest_part = [
        load(diag_h, diag, 7),
        load(off_h.at[4], off.at[4], 8),
        load(off_h.at[5], off.at[5], 9),
        load(off_h.at[0, :, :, pl.ds(1, top)], off.at[0, :, :, pl.ds(1, top)], 10),
        load(off_h.at[1, :, :, pl.ds(0, top)], off.at[1, :, :, pl.ds(0, top)], 11),
    ]
    last_part = [load(grad_h, grad, 12), load(pre_h, pre, 13), load(tip_h, tip, 14)]

    @pl.when(is_first)
    def _():
        low_d.start()
        low_w.start()

    @pl.when(jnp.logical_and(is_last, jnp.logical_not(is_first)))
    def _():
        high_d.start()
        high_w.start()

    for copy in faces + span_part + rest_part + last_part:
        copy.start()

    @pl.when(jnp.logical_not(has_left))
    def _():
        r_left[...] = jnp.zeros_like(r_left)

    @pl.when(jnp.logical_not(has_right))
    def _():
        r_right[...] = jnp.zeros_like(r_right)

    @pl.when(is_end)
    def _():
        low_d.wait()
        low_w.wait()
        axial = lax.broadcasted_iota(jnp.int32, (nx, nx), 0)

        @pl.loop(0, rows)
        def _(k):
            donors = tabd[k] & (nx - 1)
            for e in range(entries):
                hit = axial == donors[e:e + 1]
                onehot[k * entries + e] = jnp.where(hit, 1.0, 0.0).astype(jnp.bfloat16)

    row_id = lax.broadcasted_iota(jnp.int32, (rows, nx), 0)
    lane_id = lax.broadcasted_iota(jnp.int32, (rows, nx), 1)

    def product(blocks, b, i):
        total = None
        for a in range(nv):
            term = blocks(a, b)[i].astype(jnp.float32) * adj[a, i]
            total = term if total is None else total + term
        return total

    def along(d):
        return lambda a, b: off.at[d, a, b]

    def scatter():
        scat[...] = jnp.zeros_like(scat)

        @pl.loop(0, rows // UNROLL)
        def _(step):
            total = None
            for u in range(UNROLL):
                k = step * UNROLL + u
                target_rows = tabd[k] >> bits
                weights = tabw[k]
                values = [face[p, pl.ds(k, 1), :] for p in range(nv)]
                for e in range(entries):
                    here = row_id == target_rows[e:e + 1]
                    parts = []
                    for p in range(nv):
                        full = values[p] * weights[e:e + 1]
                        high = full.astype(jnp.bfloat16).astype(jnp.float32)
                        for piece in (high, full - high):
                            parts.append(jnp.where(here, piece, 0.0).astype(jnp.bfloat16))
                    left = jnp.concatenate(parts, axis=0)
                    term = lax.dot_general(
                        left, onehot[k * entries + e], (((1,), (1,)), ((), ())),
                        preferred_element_type=jnp.float32,
                    )
                    total = term if total is None else total + term
            scat[...] += total

    def scattered(p):
        at = 2 * p * rows
        return scat[at:at + rows, :] + scat[at + rows:at + 2 * rows, :]

    for it in range(ITERS):
        first = it == 0
        target = out if it == ITERS - 1 else adj

        def remote(src, dst, n, where):
            return pltpu.make_async_remote_copy(
                src_ref=src.at[it], dst_ref=dst.at[it],
                send_sem=send_sem.at[it, n], recv_sem=recv_sem.at[it, n],
                device_id=where, device_id_type=MESH,
            )

        up = remote(s_up, r_up, 0, {"pitch": above})
        down = remote(s_dn, r_dn, 1, {"pitch": below})
        to_left = remote(s_left, r_right, 2, {"span": si - 1})
        to_right = remote(s_right, r_left, 3, {"span": si + 1})

        if first:
            for copy in faces:
                copy.wait()

        @pl.loop(0, nv)
        def _(b):
            low = product(along(0), b, 0)
            high = product(along(1), b, top)
            s_dn[it, b] = low
            s_up[it, b] = high
            face[b] = jnp.where(is_first, low, high)

        if first:
            pl.semaphore_wait(barrier, 2 + has_left.astype(jnp.int32) + has_right.astype(jnp.int32))

        @pl.when(jnp.logical_not(is_last))
        def _():
            up.start()

        @pl.when(jnp.logical_not(is_first))
        def _():
            down.start()

        @pl.when(is_end)
        def _():
            scatter()

            @pl.when(is_first)
            def _():
                for p in range(nv):
                    s_dn[it, p] = scattered(p)
                down.start()

            @pl.when(is_last)
            def _():
                for p in range(nv):
                    s_up[it, p] = scattered(p)
                up.start()

        if first:
            for copy in span_part:
                copy.wait()

        @pl.loop(0, nv)
        def _(b):
            for i in range(lp):
                left = product(along(2), b, i)
                right = product(along(3), b, i)
                s_left[it, b, i:i + 1, :] = left[0:1]
                s_right[it, b, i:i + 1, :] = right[rows - 1:rows]
                acc[b, i] = (
                    jnp.where(row_id < rows - 1, pltpu.roll(left, rows - 1, 0), 0.0)
                    + jnp.where(row_id > 0, pltpu.roll(right, 1, 0), 0.0)
                )

        @pl.when(has_left)
        def _():
            to_left.start()

        @pl.when(has_right)
        def _():
            to_right.start()

        if first:
            for copy in rest_part:
                copy.wait()

        @pl.loop(0, nv)
        def _(b):
            for i in range(lp):
                total = acc[b, i] + product(lambda a, c: diag.at[a, c], b, i)
                back = product(along(4), b, i)
                ahead = product(along(5), b, i)
                total = total + jnp.where(lane_id < nx - 1, pltpu.roll(back, nx - 1, 1), 0.0)
                total = total + jnp.where(lane_id > 0, pltpu.roll(ahead, 1, 1), 0.0)
                if i < top:
                    total = total + product(along(0), b, i + 1)
                if i > 0:
                    total = total + product(along(1), b, i - 1)
                acc[b, i] = total

        if first:
            for copy in last_part:
                copy.wait()

        @pl.when(has_right)
        def _():
            to_left_in = remote(s_left, r_right, 2, {"span": si + 1})
            to_left_in.wait_recv()

        @pl.when(has_left)
        def _():
            to_right_in = remote(s_right, r_left, 3, {"span": si - 1})
            to_right_in.wait_recv()

        def finish(i):
            step = jnp.where(tip[i] == 1, 0.3, 0.6)
            rest = []
            for b in range(nv):
                total = acc[b, i] + grad[b, i]
                total = total + jnp.where(row_id == rows - 1, r_right[it, b, i:i + 1, :], 0.0)
                total = total + jnp.where(row_id == 0, r_left[it, b, i:i + 1, :], 0.0)
                if i == 0:
                    total = total + r_up[it, b]
                if i == top:
                    total = total + r_dn[it, b]
                rest.append(total)
            for a in range(nv):
                total = None
                for b in range(nv):
                    term = pre[a, b, i].astype(jnp.float32) * rest[b]
                    total = term if total is None else total + term
                target[a, i] = adj[a, i] - step * total

        for i in range(1, top):
            finish(i)
        up.wait_recv()
        if top == 0:
            down.wait_recv()
        finish(0)
        if top > 0:
            down.wait_recv()
            finish(top)

        up.wait_send()
        down.wait_send()

        @pl.when(has_left)
        def _():
            to_left.wait_send()

        @pl.when(has_right)
        def _():
            to_right.wait_send()


def body(sizes, adjoint, gradient, diag_blocks, off_blocks, precond,
         low_donor, low_weight, high_donor, high_weight, tip_mask):
    pitches, spans = sizes
    nv, lp, rows, nx = adjoint.shape
    entries = low_donor.shape[2]
    dims = (pitches, spans, nv, lp, rows, nx, entries)
    tables = [jnp.swapaxes(t, 1, 2) for t in (low_donor, low_weight, high_donor, high_weight)]
    f32 = jnp.float32
    whole = pltpu.VMEM((nv, lp, rows, nx), f32)
    pitch_face = pltpu.VMEM((ITERS, nv, rows, nx), f32)
    span_face = pltpu.VMEM((ITERS, nv, lp, nx), f32)
    return pl.pallas_call(
        functools.partial(kernel, dims),
        out_shape=jax.ShapeDtypeStruct(adjoint.shape, f32),
        in_specs=[pl.BlockSpec(memory_space=pl.ANY)] * 10,
        out_specs=pl.BlockSpec(memory_space=pltpu.VMEM),
        scratch_shapes=[
            whole, whole,
            pltpu.VMEM(diag_blocks.shape, jnp.bfloat16),
            pltpu.VMEM(off_blocks.shape, jnp.bfloat16),
            pltpu.VMEM(precond.shape, jnp.bfloat16),
            pltpu.VMEM((rows, entries, nx), jnp.int32),
            pltpu.VMEM((rows, entries, nx), f32),
            pltpu.VMEM(tip_mask.shape, jnp.int32),
            pltpu.VMEM((rows * entries, nx, nx), jnp.bfloat16),
            pltpu.VMEM((nv, rows, nx), f32),
            pltpu.VMEM((2 * nv * rows, nx), f32),
            whole,
            pitch_face, pitch_face, pitch_face, pitch_face,
            span_face, span_face, span_face, span_face,
            pltpu.SemaphoreType.DMA((15,)),
            pltpu.SemaphoreType.DMA((ITERS, 4)),
            pltpu.SemaphoreType.DMA((ITERS, 4)),
        ],
        compiler_params=pltpu.CompilerParams(
            collective_id=0, has_side_effects=True, vmem_limit_bytes=56 * 1024 * 1024
        ),
    )(adjoint, gradient, diag_blocks, off_blocks, precond, *tables, tip_mask)


def solution(mesh):
    sizes = (mesh.shape["pitch"], mesh.shape["span"])
    return jax.shard_map(
        functools.partial(body, sizes),
        mesh=mesh,
        in_specs=(
            P(None, "pitch", "span", None),
            P(None, "pitch", "span", None),
            P(None, None, "pitch", "span", None),
            P(None, None, None, "pitch", "span", None),
            P(None, None, "pitch", "span", None),
            P("span", None, None),
            P("span", None, None),
            P("span", None, None),
            P("span", None, None),
            P("pitch", "span", None),
        ),
        out_specs=P(None, "pitch", "span", None),
        check_vma=False,
    )
```

```python
import functools

import jax
import jax.numpy as jnp
from jax import lax
from jax.experimental import pallas as pl
from jax.experimental.pallas import tpu as pltpu
from jax.sharding import PartitionSpec as P

ITERS = 2
MESH = pl.DeviceIdType.MESH
UNROLL = 4
CHUNKS = 2


def kernel(
    dims,
    adj_h, grad_h, diag_h, off_h, pre_h, ld_h, lw_h, hd_h, hw_h, tip_h,
    out,
    adj, grad, diag, off, pre, tabd, tabw, tip,
    onehot, in_row, tab2, pieces, scat, acc,
    s_up, s_dn, r_up, r_dn, s_left, s_right, r_left, r_right,
    load_sem, send_sem, recv_sem,
):
    pitches, spans, nv, lp, rows, nx, entries = dims
    top = lp - 1
    bits = nx.bit_length() - 1
    pi = lax.axis_index("pitch")
    si = lax.axis_index("span")
    above = lax.rem(pi + 1, pitches)
    below = lax.rem(pi + pitches - 1, pitches)
    is_first = pi == 0
    is_last = pi == pitches - 1
    is_end = jnp.logical_or(is_first, is_last)
    has_left = si > 0
    has_right = si < spans - 1

    barrier = pltpu.get_barrier_semaphore()
    pl.semaphore_signal(barrier, inc=1, device_id={"pitch": above}, device_id_type=MESH)
    pl.semaphore_signal(barrier, inc=1, device_id={"pitch": below}, device_id_type=MESH)

    @pl.when(has_left)
    def _():
        pl.semaphore_signal(barrier, inc=1, device_id={"span": si - 1}, device_id_type=MESH)

    @pl.when(has_right)
    def _():
        pl.semaphore_signal(barrier, inc=1, device_id={"span": si + 1}, device_id_type=MESH)

    def load(src, dst, n):
        return pltpu.make_async_copy(src, dst, load_sem.at[n])

    low_d, low_w = load(ld_h, tabd, 0), load(lw_h, tabw, 1)
    high_d, high_w = load(hd_h, tabd, 0), load(hw_h, tabw, 1)
    faces = [
        load(adj_h, adj, 2),
        load(off_h.at[0, :, :, 0], off.at[0, :, :, 0], 3),
        load(off_h.at[1, :, :, top], off.at[1, :, :, top], 4),
    ]
    span_part = [load(off_h.at[2], off.at[2], 5), load(off_h.at[3], off.at[3], 6)]
    rest_part = [
        load(diag_h, diag, 7),
        load(off_h.at[4], off.at[4], 8),
        load(off_h.at[5], off.at[5], 9),
        load(off_h.at[0, :, :, pl.ds(1, top)], off.at[0, :, :, pl.ds(1, top)], 10),
        load(off_h.at[1, :, :, pl.ds(0, top)], off.at[1, :, :, pl.ds(0, top)], 11),
    ]
    last_part = [load(grad_h, grad, 12), load(pre_h, pre, 13), load(tip_h, tip, 14)]

    @pl.when(is_last)
    def _():
        low_d.start()
        low_w.start()

    @pl.when(jnp.logical_and(is_first, jnp.logical_not(is_last)))
    def _():
        high_d.start()
        high_w.start()

    for copy in faces + span_part + rest_part + last_part:
        copy.start()

    @pl.when(jnp.logical_not(has_left))
    def _():
        r_left[...] = jnp.zeros_like(r_left)

    @pl.when(jnp.logical_not(has_right))
    def _():
        r_right[...] = jnp.zeros_like(r_right)

    @pl.when(is_end)
    def _():
        low_d.wait()
        low_w.wait()
        axial = lax.broadcasted_iota(jnp.int32, (nx, nx), 0)

        span_row = lax.broadcasted_iota(jnp.int32, (rows, nx), 0)

        @pl.loop(0, rows)
        def _(k):
            donors = tabd[k]
            weights = tabw[k]
            for e in range(entries):
                hit = axial == donors[e:e + 1] & (nx - 1)
                onehot[k * entries + e] = jnp.where(hit, 1.0, 0.0).astype(jnp.bfloat16)
                here = span_row == donors[e:e + 1] >> bits
                in_row[k * entries + e] = jnp.where(here, 1.0, 0.0).astype(jnp.bfloat16)
                tab2[e, pl.ds(k, 1), :] = weights[e:e + 1]

    row_id = lax.broadcasted_iota(jnp.int32, (rows, nx), 0)
    lane_id = lax.broadcasted_iota(jnp.int32, (rows, nx), 1)

    def product(blocks, b, i):
        total = None
        for a in range(nv):
            term = blocks(a, b)[i].astype(jnp.float32) * adj[a, i]
            total = term if total is None else total + term
        return total

    def along(d):
        return lambda a, b: off.at[d, a, b]

    def scatter(it, c):
        part = rows // CHUNKS
        here = pl.ds(c * part, part)
        for p in range(nv):
            value = jnp.where(is_first, r_up[it, p, here, :], r_dn[it, p, here, :])
            for e in range(entries):
                full = value * tab2[e, here, :]
                high = full.astype(jnp.bfloat16).astype(jnp.float32)
                pieces[e, 2 * p, here, :] = high
                pieces[e, 2 * p + 1, here, :] = full - high

        @pl.loop(0, part // UNROLL)
        def _(step):
            total = None
            for u in range(UNROLL):
                k = c * part + step * UNROLL + u
                for e in range(entries):
                    mask = in_row[k * entries + e]
                    parts = []
                    for q in range(2 * nv):
                        row = jnp.broadcast_to(pieces[e, q, pl.ds(k, 1), :], (rows, nx))
                        parts.append(row.astype(jnp.bfloat16) * mask)
                    term = lax.dot_general(
                        jnp.concatenate(parts, axis=0), onehot[k * entries + e],
                        (((1,), (1,)), ((), ())), preferred_element_type=jnp.float32,
                    )
                    total = term if total is None else total + term
            scat[c] = total if part == UNROLL else scat[c] + total

    def scattered(p):
        at = 2 * p * rows
        total = None
        for c in range(CHUNKS):
            for start in (at, at + rows):
                term = scat[c, start:start + rows, :]
                total = term if total is None else total + term
        return total

    for it in range(ITERS):
        first = it == 0
        target = out if it == ITERS - 1 else adj

        def remote(src, dst, n, where):
            return pltpu.make_async_remote_copy(
                src_ref=src.at[it], dst_ref=dst.at[it],
                send_sem=send_sem.at[it, n], recv_sem=recv_sem.at[it, n],
                device_id=where, device_id_type=MESH,
            )

        def remote_part(src, dst, n, c, where):
            here = pl.ds(c * (rows // CHUNKS), rows // CHUNKS)
            return pltpu.make_async_remote_copy(
                src_ref=src.at[it, :, here], dst_ref=dst.at[it, :, here],
                send_sem=send_sem.at[it, n + c], recv_sem=recv_sem.at[it, n + c],
                device_id=where, device_id_type=MESH,
            )

        up = [remote_part(s_up, r_up, 4, c, {"pitch": above}) for c in range(CHUNKS)]
        down = [remote_part(s_dn, r_dn, 4 + CHUNKS, c, {"pitch": below}) for c in range(CHUNKS)]
        to_left = remote(s_left, r_right, 2, {"span": si - 1})
        to_right = remote(s_right, r_left, 3, {"span": si + 1})

        if first:
            for copy in faces:
                copy.wait()

        @pl.loop(0, nv)
        def _(b):
            low = product(along(0), b, 0)
            high = product(along(1), b, top)
            s_dn[it, b] = low
            s_up[it, b] = high

        if first:
            pl.semaphore_wait(barrier, 2 + has_left.astype(jnp.int32) + has_right.astype(jnp.int32))

        for c in range(CHUNKS):
            up[c].start()
            down[c].start()

        if first:
            for copy in span_part:
                copy.wait()

        @pl.loop(0, nv)
        def _(b):
            for i in range(lp):
                left = product(along(2), b, i)
                right = product(along(3), b, i)
                s_left[it, b, i:i + 1, :] = left[0:1]
                s_right[it, b, i:i + 1, :] = right[rows - 1:rows]
                acc[b, i] = (
                    jnp.where(row_id < rows - 1, pltpu.roll(left, rows - 1, 0), 0.0)
                    + jnp.where(row_id > 0, pltpu.roll(right, 1, 0), 0.0)
                )

        @pl.when(has_left)
        def _():
            to_left.start()

        @pl.when(has_right)
        def _():
            to_right.start()

        if first:
            for copy in rest_part:
                copy.wait()

        @pl.loop(0, nv)
        def _(b):
            for i in range(lp):
                total = acc[b, i] + product(lambda a, c: diag.at[a, c], b, i)
                back = product(along(4), b, i)
                ahead = product(along(5), b, i)
                total = total + jnp.where(lane_id < nx - 1, pltpu.roll(back, nx - 1, 1), 0.0)
                total = total + jnp.where(lane_id > 0, pltpu.roll(ahead, 1, 1), 0.0)
                if i < top:
                    total = total + product(along(0), b, i + 1)
                if i > 0:
                    total = total + product(along(1), b, i - 1)
                acc[b, i] = total

        if first:
            for copy in last_part:
                copy.wait()

        @pl.when(has_right)
        def _():
            to_left_in = remote(s_left, r_right, 2, {"span": si + 1})
            to_left_in.wait_recv()

        @pl.when(has_left)
        def _():
            to_right_in = remote(s_right, r_left, 3, {"span": si - 1})
            to_right_in.wait_recv()

        def finish(i):
            step = jnp.where(tip[i] == 1, 0.3, 0.6)
            rest = []
            for b in range(nv):
                total = acc[b, i] + grad[b, i]
                total = total + jnp.where(row_id == rows - 1, r_right[it, b, i:i + 1, :], 0.0)
                total = total + jnp.where(row_id == 0, r_left[it, b, i:i + 1, :], 0.0)
                if i == 0:
                    total = total + r_up[it, b]
                if i == top:
                    total = total + r_dn[it, b]
                rest.append(total)
            for a in range(nv):
                total = None
                for b in range(nv):
                    term = pre[a, b, i].astype(jnp.float32) * rest[b]
                    total = term if total is None else total + term
                target[a, i] = adj[a, i] - step * total

        for i in range(1, top):
            finish(i)
        @pl.when(is_end)
        def _():
            if rows // CHUNKS != UNROLL:
                scat[...] = jnp.zeros_like(scat)
            for c in range(CHUNKS):
                up[c].wait_recv()
                down[c].wait_recv()
                scatter(it, c)

            @pl.when(is_first)
            def _():
                for p in range(nv):
                    r_up[it, p] = scattered(p)

            @pl.when(is_last)
            def _():
                for p in range(nv):
                    r_dn[it, p] = scattered(p)

        @pl.when(jnp.logical_not(is_end))
        def _():
            for c in range(CHUNKS):
                up[c].wait_recv()
                down[c].wait_recv()

        finish(0)
        if top > 0:
            finish(top)

        for c in range(CHUNKS):
            up[c].wait_send()
            down[c].wait_send()

        @pl.when(has_left)
        def _():
            to_left.wait_send()

        @pl.when(has_right)
        def _():
            to_right.wait_send()


def body(sizes, adjoint, gradient, diag_blocks, off_blocks, precond,
         low_donor, low_weight, high_donor, high_weight, tip_mask):
    pitches, spans = sizes
    nv, lp, rows, nx = adjoint.shape
    entries = low_donor.shape[2]
    dims = (pitches, spans, nv, lp, rows, nx, entries)
    tables = [jnp.swapaxes(t, 1, 2) for t in (low_donor, low_weight, high_donor, high_weight)]
    f32 = jnp.float32
    whole = pltpu.VMEM((nv, lp, rows, nx), f32)
    pitch_face = pltpu.VMEM((ITERS, nv, rows, nx), f32)
    span_face = pltpu.VMEM((ITERS, nv, lp, nx), f32)
    return pl.pallas_call(
        functools.partial(kernel, dims),
        out_shape=pltpu.VMEM(adjoint.shape, f32),
        in_specs=[pl.BlockSpec(memory_space=pl.ANY)] * 10,
        out_specs=pl.BlockSpec(memory_space=pltpu.VMEM),
        scratch_shapes=[
            whole, whole,
            pltpu.VMEM(diag_blocks.shape, jnp.bfloat16),
            pltpu.VMEM(off_blocks.shape, jnp.bfloat16),
            pltpu.VMEM(precond.shape, jnp.bfloat16),
            pltpu.VMEM((rows, entries, nx), jnp.int32),
            pltpu.VMEM((rows, entries, nx), f32),
            pltpu.VMEM(tip_mask.shape, jnp.int32),
            pltpu.VMEM((rows * entries, nx, nx), jnp.bfloat16),
            pltpu.VMEM((rows * entries, rows, nx), jnp.bfloat16),
            pltpu.VMEM((entries, rows, nx), f32),
            pltpu.VMEM((entries, 2 * nv, rows, nx), f32),
            pltpu.VMEM((CHUNKS, 2 * nv * rows, nx), f32),
            whole,
            pitch_face, pitch_face, pitch_face, pitch_face,
            span_face, span_face, span_face, span_face,
            pltpu.SemaphoreType.DMA((15,)),
            pltpu.SemaphoreType.DMA((ITERS, 4 + 2 * CHUNKS)),
            pltpu.SemaphoreType.DMA((ITERS, 4 + 2 * CHUNKS)),
        ],
        compiler_params=pltpu.CompilerParams(
            collective_id=0, has_side_effects=True, vmem_limit_bytes=56 * 1024 * 1024
        ),
    )(adjoint, gradient, diag_blocks, off_blocks, precond, *tables, tip_mask)


def solution(mesh):
    sizes = (mesh.shape["pitch"], mesh.shape["span"])
    return jax.shard_map(
        functools.partial(body, sizes),
        mesh=mesh,
        in_specs=(
            P(None, "pitch", "span", None),
            P(None, "pitch", "span", None),
            P(None, None, "pitch", "span", None),
            P(None, None, None, "pitch", "span", None),
            P(None, None, "pitch", "span", None),
            P("span", None, None),
            P("span", None, None),
            P("span", None, None),
            P("span", None, None),
            P("pitch", "span", None),
        ),
        out_specs=P(None, "pitch", "span", None),
        check_vma=False,
    )
```

```python
import functools

import jax
import jax.numpy as jnp
from jax import lax
from jax.experimental import pallas as pl
from jax.experimental.pallas import tpu as pltpu
from jax.sharding import PartitionSpec as P

ITERS = 2
MESH = pl.DeviceIdType.MESH
UNROLL = 16
CHUNKS = 1


def kernel(
    dims,
    adj_h, grad_h, diag_h, off_h, pre_h, ld_h, lw_h, hd_h, hw_h, tip_h,
    out,
    adj, grad, diag, off, pre, tabd, tabw, tip,
    onehot, in_row, tab2, pieces, scat, acc,
    s_up, s_dn, r_up, r_dn, s_left, s_right, r_left, r_right,
    load_sem, send_sem, recv_sem,
):
    pitches, spans, nv, lp, rows, nx, entries = dims
    top = lp - 1
    bits = nx.bit_length() - 1
    pi = lax.axis_index("pitch")
    si = lax.axis_index("span")
    above = lax.rem(pi + 1, pitches)
    below = lax.rem(pi + pitches - 1, pitches)
    is_first = pi == 0
    is_last = pi == pitches - 1
    is_end = jnp.logical_or(is_first, is_last)
    has_left = si > 0
    has_right = si < spans - 1

    barrier = pltpu.get_barrier_semaphore()
    pl.semaphore_signal(barrier, inc=1, device_id={"pitch": above}, device_id_type=MESH)
    pl.semaphore_signal(barrier, inc=1, device_id={"pitch": below}, device_id_type=MESH)

    @pl.when(has_left)
    def _():
        pl.semaphore_signal(barrier, inc=1, device_id={"span": si - 1}, device_id_type=MESH)

    @pl.when(has_right)
    def _():
        pl.semaphore_signal(barrier, inc=1, device_id={"span": si + 1}, device_id_type=MESH)

    def load(src, dst, n):
        return pltpu.make_async_copy(src, dst, load_sem.at[n])

    low_d, low_w = load(ld_h, tabd, 0), load(lw_h, tabw, 1)
    high_d, high_w = load(hd_h, tabd, 0), load(hw_h, tabw, 1)
    faces = [
        load(adj_h, adj, 2),
        load(off_h.at[0, :, :, 0], off.at[0, :, :, 0], 3),
        load(off_h.at[1, :, :, top], off.at[1, :, :, top], 4),
    ]
    span_part = [load(off_h.at[2], off.at[2], 5), load(off_h.at[3], off.at[3], 6)]
    rest_part = [
        load(diag_h, diag, 7),
        load(off_h.at[4], off.at[4], 8),
        load(off_h.at[5], off.at[5], 9),
        load(off_h.at[0, :, :, pl.ds(1, top)], off.at[0, :, :, pl.ds(1, top)], 10),
        load(off_h.at[1, :, :, pl.ds(0, top)], off.at[1, :, :, pl.ds(0, top)], 11),
    ]
    last_part = [load(grad_h, grad, 12), load(pre_h, pre, 13), load(tip_h, tip, 14)]

    @pl.when(is_last)
    def _():
        low_d.start()
        low_w.start()

    @pl.when(jnp.logical_and(is_first, jnp.logical_not(is_last)))
    def _():
        high_d.start()
        high_w.start()

    for copy in faces + span_part + rest_part + last_part:
        copy.start()

    @pl.when(jnp.logical_not(has_left))
    def _():
        r_left[...] = jnp.zeros_like(r_left)

    @pl.when(jnp.logical_not(has_right))
    def _():
        r_right[...] = jnp.zeros_like(r_right)

    @pl.when(is_end)
    def _():
        low_d.wait()
        low_w.wait()
        axial = lax.broadcasted_iota(jnp.int32, (nx, nx), 0)

        span_row = lax.broadcasted_iota(jnp.int32, (rows, nx), 0)

        @pl.loop(0, rows)
        def _(k):
            donors = tabd[k]
            weights = tabw[k]
            for e in range(entries):
                hit = axial == donors[e:e + 1] & (nx - 1)
                onehot[k * entries + e] = jnp.where(hit, 1.0, 0.0).T.astype(jnp.bfloat16)
                here = span_row == donors[e:e + 1] >> bits
                in_row[k * entries + e] = jnp.where(here, 1.0, 0.0).astype(jnp.bfloat16)
                tab2[e, pl.ds(k, 1), :] = weights[e:e + 1]

    row_id = lax.broadcasted_iota(jnp.int32, (rows, nx), 0)
    lane_id = lax.broadcasted_iota(jnp.int32, (rows, nx), 1)

    def product(blocks, b, i):
        total = None
        for a in range(nv):
            term = blocks(a, b)[i].astype(jnp.float32) * adj[a, i]
            total = term if total is None else total + term
        return total

    def along(d):
        return lambda a, b: off.at[d, a, b]

    def scatter(it, c):
        part = rows // CHUNKS
        here = pl.ds(c * part, part)
        for p in range(nv):
            value = jnp.where(is_first, r_up[it, p, here, :], r_dn[it, p, here, :])
            for e in range(entries):
                full = value * tab2[e, here, :]
                high = full.astype(jnp.bfloat16).astype(jnp.float32)
                pieces[e, 2 * p, here, :] = high
                pieces[e, 2 * p + 1, here, :] = full - high

        @pl.loop(0, part // UNROLL)
        def _(step):
            total = None
            for u in range(UNROLL):
                k = c * part + step * UNROLL + u
                for e in range(entries):
                    mask = in_row[k * entries + e]
                    parts = []
                    for q in range(2 * nv):
                        row = jnp.broadcast_to(pieces[e, q, pl.ds(k, 1), :], (rows, nx))
                        parts.append(row.astype(jnp.bfloat16) * mask)
                    term = lax.dot_general(
                        jnp.concatenate(parts, axis=0), onehot[k * entries + e],
                        (((1,), (0,)), ((), ())), preferred_element_type=jnp.float32,
                    )
                    total = term if total is None else total + term
            scat[c] = total if part == UNROLL else scat[c] + total

    def scattered(p):
        at = 2 * p * rows
        total = None
        for c in range(CHUNKS):
            for start in (at, at + rows):
                term = scat[c, start:start + rows, :]
                total = term if total is None else total + term
        return total

    for it in range(ITERS):
        first = it == 0
        target = out if it == ITERS - 1 else adj

        def remote(src, dst, n, where):
            return pltpu.make_async_remote_copy(
                src_ref=src.at[it], dst_ref=dst.at[it],
                send_sem=send_sem.at[it, n], recv_sem=recv_sem.at[it, n],
                device_id=where, device_id_type=MESH,
            )

        def remote_part(src, dst, n, c, where):
            here = pl.ds(c * (rows // CHUNKS), rows // CHUNKS)
            return pltpu.make_async_remote_copy(
                src_ref=src.at[it, :, here], dst_ref=dst.at[it, :, here],
                send_sem=send_sem.at[it, n + c], recv_sem=recv_sem.at[it, n + c],
                device_id=where, device_id_type=MESH,
            )

        up = [remote_part(s_up, r_up, 4, c, {"pitch": above}) for c in range(CHUNKS)]
        down = [remote_part(s_dn, r_dn, 4 + CHUNKS, c, {"pitch": below}) for c in range(CHUNKS)]
        to_left = remote(s_left, r_right, 2, {"span": si - 1})
        to_right = remote(s_right, r_left, 3, {"span": si + 1})

        if first:
            for copy in faces:
                copy.wait()

        @pl.loop(0, nv)
        def _(b):
            low = product(along(0), b, 0)
            high = product(along(1), b, top)
            s_dn[it, b] = low
            s_up[it, b] = high

        if first:
            pl.semaphore_wait(barrier, 2 + has_left.astype(jnp.int32) + has_right.astype(jnp.int32))

        @pl.when(is_first)
        def _():
            for c in range(CHUNKS):
                down[c].start()

        @pl.when(jnp.logical_not(is_first))
        def _():
            for c in range(CHUNKS):
                up[c].start()

        @pl.when(jnp.logical_not(is_end))
        def _():
            for c in range(CHUNKS):
                down[c].start()


        if first:
            for copy in span_part:
                copy.wait()

        @pl.loop(0, nv)
        def _(b):
            for i in range(lp):
                left = product(along(2), b, i)
                right = product(along(3), b, i)
                s_left[it, b, i:i + 1, :] = left[0:1]
                s_right[it, b, i:i + 1, :] = right[rows - 1:rows]
                acc[b, i] = (
                    jnp.where(row_id < rows - 1, pltpu.roll(left, rows - 1, 0), 0.0)
                    + jnp.where(row_id > 0, pltpu.roll(right, 1, 0), 0.0)
                )

        @pl.when(has_left)
        def _():
            to_left.start()

        @pl.when(has_right)
        def _():
            to_right.start()

        if first:
            for copy in rest_part:
                copy.wait()

        @pl.loop(0, nv)
        def _(b):
            for i in range(lp):
                total = acc[b, i] + product(lambda a, c: diag.at[a, c], b, i)
                back = product(along(4), b, i)
                ahead = product(along(5), b, i)
                total = total + jnp.where(lane_id < nx - 1, pltpu.roll(back, nx - 1, 1), 0.0)
                total = total + jnp.where(lane_id > 0, pltpu.roll(ahead, 1, 1), 0.0)
                if i < top:
                    total = total + product(along(0), b, i + 1)
                if i > 0:
                    total = total + product(along(1), b, i - 1)
                acc[b, i] = total

        @pl.when(is_first)
        def _():
            for c in range(CHUNKS):
                up[c].start()

        @pl.when(is_last)
        def _():
            for c in range(CHUNKS):
                down[c].start()

        if first:
            for copy in last_part:
                copy.wait()

        @pl.when(has_right)
        def _():
            to_left_in = remote(s_left, r_right, 2, {"span": si + 1})
            to_left_in.wait_recv()

        @pl.when(has_left)
        def _():
            to_right_in = remote(s_right, r_left, 3, {"span": si - 1})
            to_right_in.wait_recv()

        def finish(i):
            step = jnp.where(tip[i] == 1, 0.3, 0.6)
            rest = []
            for b in range(nv):
                total = acc[b, i] + grad[b, i]
                total = total + jnp.where(row_id == rows - 1, r_right[it, b, i:i + 1, :], 0.0)
                total = total + jnp.where(row_id == 0, r_left[it, b, i:i + 1, :], 0.0)
                if i == 0:
                    total = total + r_up[it, b]
                if i == top:
                    total = total + r_dn[it, b]
                rest.append(total)
            for a in range(nv):
                total = None
                for b in range(nv):
                    term = pre[a, b, i].astype(jnp.float32) * rest[b]
                    total = term if total is None else total + term
                target[a, i] = adj[a, i] - step * total

        for i in range(1, top):
            finish(i)
        @pl.when(is_end)
        def _():
            if rows // CHUNKS != UNROLL:
                scat[...] = jnp.zeros_like(scat)
            for c in range(CHUNKS):
                up[c].wait_recv()
                down[c].wait_recv()
                scatter(it, c)

            @pl.when(is_first)
            def _():
                for p in range(nv):
                    r_up[it, p] = scattered(p)

            @pl.when(is_last)
            def _():
                for p in range(nv):
                    r_dn[it, p] = scattered(p)

        @pl.when(jnp.logical_not(is_end))
        def _():
            for c in range(CHUNKS):
                up[c].wait_recv()
                down[c].wait_recv()

        finish(0)
        if top > 0:
            finish(top)

        for c in range(CHUNKS):
            up[c].wait_send()
            down[c].wait_send()

        @pl.when(has_left)
        def _():
            to_left.wait_send()

        @pl.when(has_right)
        def _():
            to_right.wait_send()


def body(sizes, adjoint, gradient, diag_blocks, off_blocks, precond,
         low_donor, low_weight, high_donor, high_weight, tip_mask):
    pitches, spans = sizes
    nv, lp, rows, nx = adjoint.shape
    entries = low_donor.shape[2]
    dims = (pitches, spans, nv, lp, rows, nx, entries)
    tables = [jnp.swapaxes(t, 1, 2) for t in (low_donor, low_weight, high_donor, high_weight)]
    f32 = jnp.float32
    whole = pltpu.VMEM((nv, lp, rows, nx), f32)
    pitch_face = pltpu.VMEM((ITERS, nv, rows, nx), f32)
    span_face = pltpu.VMEM((ITERS, nv, lp, nx), f32)
    return pl.pallas_call(
        functools.partial(kernel, dims),
        out_shape=pltpu.VMEM(adjoint.shape, f32),
        in_specs=[pl.BlockSpec(memory_space=pl.ANY)] * 10,
        out_specs=pl.BlockSpec(memory_space=pltpu.VMEM),
        scratch_shapes=[
            whole, whole,
            pltpu.VMEM(diag_blocks.shape, jnp.bfloat16),
            pltpu.VMEM(off_blocks.shape, jnp.bfloat16),
            pltpu.VMEM(precond.shape, jnp.bfloat16),
            pltpu.VMEM((rows, entries, nx), jnp.int32),
            pltpu.VMEM((rows, entries, nx), f32),
            pltpu.VMEM(tip_mask.shape, jnp.int32),
            pltpu.VMEM((rows * entries, nx, nx), jnp.bfloat16),
            pltpu.VMEM((rows * entries, rows, nx), jnp.bfloat16),
            pltpu.VMEM((entries, rows, nx), f32),
            pltpu.VMEM((entries, 2 * nv, rows, nx), f32),
            pltpu.VMEM((CHUNKS, 2 * nv * rows, nx), f32),
            whole,
            pitch_face, pitch_face, pitch_face, pitch_face,
            span_face, span_face, span_face, span_face,
            pltpu.SemaphoreType.DMA((15,)),
            pltpu.SemaphoreType.DMA((ITERS, 4 + 2 * CHUNKS)),
            pltpu.SemaphoreType.DMA((ITERS, 4 + 2 * CHUNKS)),
        ],
        compiler_params=pltpu.CompilerParams(
            collective_id=0, has_side_effects=True, vmem_limit_bytes=56 * 1024 * 1024
        ),
    )(adjoint, gradient, diag_blocks, off_blocks, precond, *tables, tip_mask)


def solution(mesh):
    sizes = (mesh.shape["pitch"], mesh.shape["span"])
    return jax.shard_map(
        functools.partial(body, sizes),
        mesh=mesh,
        in_specs=(
            P(None, "pitch", "span", None),
            P(None, "pitch", "span", None),
            P(None, None, "pitch", "span", None),
            P(None, None, None, "pitch", "span", None),
            P(None, None, "pitch", "span", None),
            P("span", None, None),
            P("span", None, None),
            P("span", None, None),
            P("span", None, None),
            P("pitch", "span", None),
        ),
        out_specs=P(None, "pitch", "span", None),
        check_vma=False,
    )
```
